512 devices in a mesh: row: 16 (over y, core), col: 32 (over x, z).
Axes of the slice: x: 4, y: 8, z: 8, core: 2. Of those that a mesh axis runs over, the one named last changes fastest.
Arguments:
- val_waves: bfloat16 [2, 16, 64, 4096], P(None, 'row', 'col'), may hold values from -6 to 6
- cond_waves: bfloat16 [2, 64, 64, 4096], P(None, 'row', 'col'), may hold values from -6 to 6
- val_energy: float32 [16], replicated, may hold values from -6 to -0.5
- cond_energy: float32 [64], replicated, may hold values from 0.5 to 12
- val_index: int32 [512], replicated, may hold values from 0 to 15
- cond_index: int32 [512], replicated, may hold values from 0 to 63
- grid_index: int32 [16384], replicated, may hold values from 0 to 262143, as said below
Outputs:
- chi_zero: float32 [2, 16384, 16384], P(None, 'row', 'col')
The draws below stay inside these ranges and needn't reach their ends.
Inputs may be any that keep to these rules, and one draw needn't show every extreme that they name: `grid_index`: all entries are different.
All inputs are finite; a program needn't handle non-finite values.
Results may differ from the reference program's by a relative error of at most 0.004.
Values may be sent and summed in bfloat16 or wider, within the bound.
A program may use at most 64 MiB of HBM per device.

```python
import jax
import jax.numpy as jnp
from jax import lax

GRID = 64
NG = 16384
PAIRS = 512
VB = 16
CB = 64


def draw_grid_index(key, part):
    key = jax.random.fold_in(key, 11)
    total_points = GRID ** 3
    inner_points = jax.random.permutation(jax.random.fold_in(key, 1), total_points - 2)[:NG - 2] + 1
    full_points = jnp.concatenate([jnp.zeros((1,), jnp.int32), inner_points.astype(jnp.int32), jnp.full((1,), total_points - 1, jnp.int32)])
    ordering = jax.random.permutation(jax.random.fold_in(key, 2), NG)
    return full_points[ordering]


def set_ends(values, own_key, low, high):
    dims = values.shape
    spot = [jax.random.randint(jax.random.fold_in(own_key, axis), (), 0, dims[axis]) for axis in range(len(dims))]
    values = values.at[tuple(spot)].set(low)
    longest = dims.index(max(dims))
    spot[longest] = (spot[longest] + 1) % dims[longest]
    return values.at[tuple(spot)].set(high)


def shard_levels(key, extent, pieces, least, largest):
    def one(dim, parts):
        draws = jax.random.uniform(jax.random.fold_in(jax.random.fold_in(key, 6), dim), (parts,), jnp.float32, least / len(pieces), largest / len(pieces))
        return jnp.repeat(jnp.exp(draws), extent[dim] // parts).reshape((-1,) + (1,) * (len(extent) - dim - 1))

    level = one(*pieces[0])
    for cut in pieces[1:]:
        level = level * one(*cut)
    return level


def scatter_about(key, shape, scale, most, shards=(), kind=jnp.bfloat16):
    values = jax.random.normal(key, shape, jnp.float32) * scale
    if len(shards) > 0:
        values = shard_levels(key, shape, shards, -0.22, 0.18) * values
    return jnp.clip(values, min=-most, max=most).astype(kind)


def setup_inputs(seed: int = 0) -> dict:
    key_list = jax.random.split(jax.random.key(seed), 8)
    return {
        "val_waves": scatter_about(key_list[0], (2, VB, GRID, GRID * GRID), 1.0, 6.0, ((1, 16), (2, 32))),
        "cond_waves": scatter_about(key_list[1], (2, CB, GRID, GRID * GRID), 1.0, 6.0, ((1, 16), (2, 32))),
        "val_energy": jnp.clip(jax.random.uniform(key_list[2], (VB,), jnp.float32, -6.0, -0.5), -6.0, -0.5),
        "cond_energy": jnp.clip(jax.random.uniform(key_list[3], (CB,), jnp.float32, 0.5, 12.0), 0.5, 12.0),
        "val_index": set_ends(jax.random.randint(key_list[4], (PAIRS,), 0, VB), jax.random.fold_in(key_list[4], 1), 0, VB - 1).astype(jnp.int32),
        "cond_index": set_ends(jax.random.randint(key_list[5], (PAIRS,), 0, CB), jax.random.fold_in(key_list[5], 1), 0, CB - 1).astype(jnp.int32),
        "grid_index": draw_grid_index(jax.random.fold_in(key_list[7], 71), 0),
    }


def reference(val_waves, cond_waves, val_energy, cond_energy, val_index, cond_index, grid_index):
    weight = 4.0 / (cond_energy[cond_index] - val_energy[val_index])
    factor = jnp.sqrt(weight) / GRID ** 1.5
    block_size = 16
    val_blocks = val_index.reshape(PAIRS // block_size, block_size)
    cond_blocks = cond_index.reshape(PAIRS // block_size, block_size)
    factor_blocks = factor.reshape(PAIRS // block_size, block_size)

    def one_block(inputs):
        val_sel, cond_sel, scale_sel = inputs
        valence = val_waves[:, val_sel].astype(jnp.float32)
        conduction = cond_waves[:, cond_sel].astype(jnp.float32)
        real_part = valence[0] * conduction[0] + valence[1] * conduction[1]
        imag_part = valence[0] * conduction[1] - valence[1] * conduction[0]
        density = (real_part + 1j * imag_part) * scale_sel[:, None, None]
        density = density.reshape(block_size, GRID, GRID, GRID)
        spectrum = jnp.fft.fftn(density, axes=(1, 2, 3)).reshape(block_size, GRID ** 3)
        chosen = spectrum[:, grid_index]
        return jnp.stack([jnp.real(chosen), jnp.imag(chosen)])
    spectra = lax.map(one_block, (val_blocks, cond_blocks, factor_blocks))
    spectra = jnp.transpose(spectra, (1, 0, 2, 3)).reshape(2, PAIRS, NG)
    amplitude = spectra.astype(jnp.bfloat16)
    joined = jnp.concatenate([amplitude[0], amplitude[1]], axis=0)
    swapped = jnp.concatenate([amplitude[1], -amplitude[0]], axis=0)
    joined = lax.optimization_barrier(joined).astype(jnp.float32)
    swapped = lax.optimization_barrier(swapped).astype(jnp.float32)
    scale_out = -1.0 / PAIRS
    real_out = jnp.dot(joined.T, joined, preferred_element_type=jnp.float32, precision=lax.Precision.HIGHEST) * scale_out
    imag_out = jnp.dot(swapped.T, joined, preferred_element_type=jnp.float32, precision=lax.Precision.HIGHEST) * scale_out
    return jnp.stack([real_out, imag_out])
```

```python
import functools
import math

import jax
import jax.numpy as jnp
import numpy as np
from jax import lax
from jax.experimental import pallas as pl
from jax.experimental.pallas import tpu as pltpu
from jax.sharding import PartitionSpec as P

GRID = 64
ROWS = 16
COLS = 32
CHIPS_Y = 8
CHIPS_X = 4
CHIPS_Z = 8
BANDS_DEV = 5
VMEM = pl.BlockSpec(memory_space=pltpu.VMEM)
SMEM = pl.BlockSpec(memory_space=pltpu.SMEM)
MESH = pl.DeviceIdType.MESH
VMEM_LIMIT = 56 * 1024 * 1024


def remote(src, dst, send, recv, **where):
    return pltpu.make_async_remote_copy(
        src_ref=src, dst_ref=dst, send_sem=send, recv_sem=recv,
        device_id=where, device_id_type=MESH,
    )


def greet(peers):
    barrier = pltpu.get_barrier_semaphore()
    for where in peers:
        pl.semaphore_signal(barrier, inc=1, device_id=where, device_id_type=MESH)
    pl.semaphore_wait(barrier, len(peers))


class RowGather:
    def __init__(self, own, buffer, send, recv):
        r = lax.axis_index("row")
        self.y, self.core = r // 2, r % 2
        self.own, self.buffer, self.send, self.recv = own, buffer, send, recv

    def slot(self, step, core=None):
        y = lax.rem(self.y + step + CHIPS_Y, CHIPS_Y)
        return y * 2 + (self.core if core is None else core)

    def copy(self, number, step, target):
        at = self.slot(step)
        src = self.own if step == 0 else self.buffer.at[at]
        return remote(src, self.buffer.at[at], self.send.at[number], self.recv.at[number], row=target)

    def right(self, step):
        return self.copy(step, -step, self.slot(1))

    def left(self, step):
        return self.copy(4 + step, step, self.slot(-1))

    def mate(self, step):
        return self.copy(7 + (step % CHIPS_Y), step, self.slot(0, 1 - self.core))

    def start(self):
        self.right(0).start()
        self.left(0).start()
        self.mate(0).start()

    def turn(self, step):
        self.right(step - 1).wait_recv()
        if step < 4:
            self.right(step).start()
        self.mate(-step).start()
        if step < 4:
            self.left(step - 1).wait_recv()
            if step < 3:
                self.left(step).start()
            self.mate(step).start()

    def finish(self):
        for step in range(-4, 4):
            self.mate(step).wait()
        for step in range(4):
            self.right(step).wait_send()
        for step in range(3):
            self.left(step).wait_send()


def density_kernel(val_slot, cond_slot, factor, own, out, bands, staged, ring_send, ring_recv, send, recv):
    r, c = lax.axis_index("row"), lax.axis_index("col")
    y, core = r // 2, r % 2
    row_peers = [
        lax.rem(y + 1, CHIPS_Y) * 2 + core, lax.rem(y + CHIPS_Y - 1, CHIPS_Y) * 2 + core, y * 2 + 1 - core
    ]
    greet([{"row": p} for p in row_peers] + [{"col": lax.rem(c + k, COLS)} for k in range(1, COLS)])
    gather = RowGather(own, bands, ring_send, ring_recv)
    gather.start()
    bands[r] = own[...]
    for step in range(1, 5):
        gather.turn(step)
    gather.finish()

    lane = lax.broadcasted_iota(jnp.int32, (128, 128), 1)

    def density(pair):
        bra = bands[val_slot[pair, 0], 0].astype(jnp.float32)
        ket = bands[cond_slot[pair, 0], cond_slot[pair, 1]].astype(jnp.float32)
        same = bra * ket
        cross = bra * pltpu.roll(ket, 64, 1)
        real = same + pltpu.roll(same, 64, 1)
        imag = pltpu.roll(cross, 64, 1) - cross
        return (jnp.where(lane < 64, real, imag) * factor[pair]).astype(jnp.bfloat16)

    def push(k):
        to = lax.rem(c + k, COLS)
        return remote(staged.at[to], out.at[c], send.at[k], recv.at[k], col=to)

    def produce(k, _):
        to = lax.rem(c + k, COLS)
        staged[to] = density(to)
        push(k).start()
        return 0

    lax.fori_loop(1, COLS, produce, 0)
    out[c] = density(c)

    def settle(k, _):
        origin = lax.rem(c - k + COLS, COLS)
        remote(staged.at[origin], out.at[origin], send.at[k], recv.at[k], col=origin).wait_recv()
        push(k).wait_send()
        return 0

    lax.fori_loop(1, COLS, settle, 0)


def pair_densities(val_slot, cond_slot, factor, own):
    return pl.pallas_call(
        density_kernel,
        out_shape=jax.ShapeDtypeStruct((COLS, 128, 128), jnp.bfloat16),
        in_specs=[SMEM, SMEM, SMEM, VMEM],
        out_specs=VMEM,
        scratch_shapes=[
            pltpu.VMEM((ROWS, BANDS_DEV, 128, 128), jnp.bfloat16),
            pltpu.VMEM((COLS, 128, 128), jnp.bfloat16),
            pltpu.SemaphoreType.DMA((15,)),
            pltpu.SemaphoreType.DMA((15,)),
            pltpu.SemaphoreType.DMA((COLS,)),
            pltpu.SemaphoreType.DMA((COLS,)),
        ],
        compiler_params=pltpu.CompilerParams(
            collective_id=0, has_side_effects=True, vmem_limit_bytes=VMEM_LIMIT
        ),
        name="pair_densities",
    )(val_slot, cond_slot, factor, own)


def tables():
    angle = 2.0 * math.pi / GRID * (np.outer(np.arange(GRID), np.arange(GRID)) % GRID)
    cos, sin = np.cos(angle), np.sin(angle)

    def split(table):
        high = table.astype(jnp.bfloat16)
        low = (table - high.astype(np.float64)).astype(jnp.bfloat16)
        return high, low

    z_high, z_low = split(np.block([[cos, -sin], [sin, cos]]))
    left_high, left_low = split(np.concatenate([cos, sin], axis=0))
    z_table = np.concatenate([z_high, z_low], axis=0)
    left_table = np.concatenate([left_high, left_low, left_high], axis=1)
    return jnp.asarray(z_table), jnp.asarray(left_table)


def spectrum_kernel(dens, z_table, left_table, index, amp_rows, amp_cols, first, second, picked, block):
    z_tab = z_table[...]
    left_tab = left_table[...]
    sign = jnp.where(lax.broadcasted_iota(jnp.int32, (64, 128), 1) < 64, 1.0, -1.0)

    def along_z(i, _):
        part = dens[pl.ds(i * 4, 4)].reshape(512, 128)
        wide = jnp.concatenate([part, part], axis=1)
        first[pl.ds(pl.multiple_of(i * 512, 512), 512), :] = jnp.dot(
            wide, z_tab, preferred_element_type=jnp.float32
        )
        return 0

    lax.fori_loop(0, 8, along_z, 0)

    def transform(parts):
        high = [p.astype(jnp.bfloat16) for p in parts]
        low = [(p - h.astype(jnp.float32)).astype(jnp.bfloat16) for p, h in zip(parts, high)]
        high = jnp.concatenate(high, axis=1)
        low = jnp.concatenate(low, axis=1)
        got = jnp.dot(
            left_tab, jnp.concatenate([high, high, low], axis=0), preferred_element_type=jnp.float32
        )
        return [
            got[:64, 128 * n : 128 * (n + 1)]
            + sign * pltpu.roll(got[64:, 128 * n : 128 * (n + 1)], 64, 1)
            for n in range(len(parts))
        ]

    def along_y(i, _):
        base = pl.multiple_of(i * 512, 512)
        parts = [first[pl.ds(base + 64 * n, 64), :] for n in range(8)]
        for n, part in enumerate(transform(parts)):
            second[pl.ds(base + 64 * n, 64), :] = part
        return 0

    lax.fori_loop(0, 8, along_y, 0)

    for i in range(8):
        parts = [second[pl.ds(i * 8 + n, 64, stride=64), :] for n in range(8)]
        done = transform(parts)
        for n in range(4):
            tile = jnp.concatenate(done[2 * n : 2 * n + 2], axis=0)
            number = i * 4 + n
            picked[
                pl.ds((number // 8) * 128, 128), pl.ds((number % 8) * 128, 128)
            ] = tile.T.astype(jnp.bfloat16)

    inner = lax.broadcasted_iota(jnp.int32, (1024, 1024), 0)
    outer = lax.broadcasted_iota(jnp.int32, (256, 1024), 0)

    def select(t, _):
        spot = index[pl.ds(t, 1), :]
        kx, ky, kz = spot // 4096, (spot // 64) % 64, spot % 64
        hot = jnp.where(inner == (ky % 16) * 64 + kx, 1.0, 0.0).astype(jnp.bfloat16)
        got = jnp.dot(picked[...], hot, preferred_element_type=jnp.float32)
        keep = outer == (ky // 16) * 64 + kz
        for part in range(2):
            half = jnp.concatenate(
                [got[128 * g + 64 * part : 128 * g + 64 * part + 64] for g in range(4)], axis=0
            )
            row = jnp.sum(jnp.where(keep, half, 0.0), axis=0, keepdims=True)
            for j in range(8):
                piece = row[:, 128 * j : 128 * (j + 1)]
                block[pl.ds(8 * part + j, 1), :] = piece
                amp_cols[2 * t + j // 4, pl.ds(4 * part + j % 4, 1), :] = piece
        amp_rows[t] = block[...].astype(jnp.bfloat16)
        return 0

    lax.fori_loop(0, 16, select, 0)


def spectrum(dens, index):
    z_table, left_table = tables()
    return pl.pallas_call(
        spectrum_kernel,
        out_shape=(
            jax.ShapeDtypeStruct((ROWS, 16, 128), jnp.bfloat16),
            jax.ShapeDtypeStruct((COLS, 8, 128), jnp.float32),
        ),
        in_specs=[VMEM] * 4,
        out_specs=(VMEM, VMEM),
        scratch_shapes=[
            pltpu.VMEM((4096, 128), jnp.float32),
            pltpu.VMEM((4096, 128), jnp.float32),
            pltpu.VMEM((512, 1024), jnp.bfloat16),
            pltpu.VMEM((16, 128), jnp.float32),
        ],
        compiler_params=pltpu.CompilerParams(vmem_limit_bytes=VMEM_LIMIT),
        name="spectrum",
    )(dens, z_table, left_table, index.reshape(16, 1024))


def exchange_kernel(
    amp_rows, amp_cols, left, right,
    row_land, row_wide, col_land, row_send, row_recv, col_send, col_recv,
    c_send, c_recv, a_send, a_recv, b_send, b_recv,
):
    r, c = lax.axis_index("row"), lax.axis_index("col")
    x, z = c // CHIPS_Z, c % CHIPS_Z
    greet(
        [{"row": lax.rem(r + k, ROWS)} for k in range(1, ROWS)]
        + [{"col": lax.rem(c + k, COLS)} for k in range(1, COLS)]
    )

    def row_push(k):
        to = lax.rem(r + k, ROWS)
        return remote(amp_rows.at[to], row_land.at[r], row_send.at[k], row_recv.at[k], row=to)

    def col_push(k):
        to = lax.rem(c + k, COLS)
        return remote(
            amp_cols.at[to], col_land.at[pl.ds(pl.multiple_of(c * 8, 8), 8)],
            col_send.at[k], col_recv.at[k], col=to,
        )

    def row_begin(k, _):
        row_push(k).start()
        return 0

    def col_begin(k, _):
        col_push(k).start()
        return 0

    lax.fori_loop(1, ROWS, row_begin, 0)
    lax.fori_loop(1, COLS, col_begin, 0)
    row_land[r] = amp_rows[r]
    col_land[pl.ds(pl.multiple_of(c * 8, 8), 8), :] = amp_cols[c]

    def row_settle(k, _):
        origin = lax.rem(r - k + ROWS, ROWS)
        remote(
            amp_rows.at[origin], row_land.at[origin], row_send.at[k], row_recv.at[k], row=origin
        ).wait_recv()
        return 0

    def col_settle(k, _):
        origin = lax.rem(c - k + COLS, COLS)
        remote(
            amp_cols.at[origin], col_land.at[pl.ds(pl.multiple_of(origin * 8, 8), 8)],
            col_send.at[k], col_recv.at[k], col=origin,
        ).wait_recv()
        return 0

    lax.fori_loop(1, ROWS, row_settle, 0)
    row_wide[...] = row_land[...].astype(jnp.float32).reshape(256, 128)
    for j in range(16):
        left[x, z, j] = row_wide[pl.ds(j, 16, stride=16), :].astype(jnp.bfloat16)

    def x_at(step):
        return lax.rem(x + step + CHIPS_X, CHIPS_X)

    def z_at(step):
        return lax.rem(z + step + CHIPS_Z, CHIPS_Z)

    def a_z(number, step, toward):
        ref = left.at[x, z_at(step), pl.ds(0, 8)]
        return remote(ref, ref, a_send.at[number], a_recv.at[number], col=x * CHIPS_Z + z_at(toward))

    def a_right(step):
        return a_z(step, -step, 1)

    def a_left(step):
        return a_z(4 + step, step, -1)

    def a_x(number, step, toward, low, count):
        ref = left.at[x_at(step), pl.ds(low, count), pl.ds(0, 8)]
        return remote(ref, ref, a_send.at[number], a_recv.at[number], col=x_at(toward) * CHIPS_Z + z)

    def b_x(number, toward):
        ref = left.at[x, z, pl.ds(8, 8)]
        return remote(ref, ref, b_send.at[number], b_recv.at[number], col=x_at(toward) * CHIPS_Z + z)

    def b_z(number, step, toward):
        ref = left.at[:, z_at(step), pl.ds(8, 8)]
        return remote(ref, ref, b_send.at[number], b_recv.at[number], col=x * CHIPS_Z + z_at(toward))

    def b_right(step):
        return b_z(step, -step, 1)

    def b_left(step):
        return b_z(4 + step, step, -1)

    for number, toward in ((7, 1), (8, -1), (9, 2)):
        b_x(number, toward).start()
    a_right(0).start()
    a_left(0).start()

    lax.fori_loop(1, COLS, col_settle, 0)
    for q in range(8):
        right[r, q] = col_land[pl.ds(q, 32, stride=8), :].astype(jnp.bfloat16)
    gather = RowGather(right.at[r], right, c_send, c_recv)
    gather.start()

    for number, toward in ((7, 1), (8, -1), (9, 2)):
        b_x(number, toward).wait_recv()
    b_right(0).start()
    b_left(0).start()
    for step in range(1, 5):
        a_right(step - 1).wait_recv()
        if step < 4:
            a_right(step).start()
            a_left(step - 1).wait_recv()
            if step < 3:
                a_left(step).start()
        if step < 4:
            gather.turn(step)
    across = [a_x(7, 0, 1, 0, 8), a_x(8, 0, -1, 0, 8), a_x(9, -1, 1, 0, 4), a_x(10, 1, -1, 4, 4)]
    across[0].start()
    across[1].start()
    gather.turn(4)
    for step in range(1, 5):
        b_right(step - 1).wait_recv()
        if step < 4:
            b_right(step).start()
            b_left(step - 1).wait_recv()
            if step < 3:
                b_left(step).start()
        if step == 2:
            across[0].wait_recv()
            across[2].start()
            across[1].wait_recv()
            across[3].start()
    across[2].wait_recv()
    across[3].wait_recv()

    gather.finish()
    for step in range(4):
        a_right(step).wait_send()
        b_right(step).wait_send()
    for step in range(3):
        a_left(step).wait_send()
        b_left(step).wait_send()
    for number, toward in ((7, 1), (8, -1), (9, 2)):
        b_x(number, toward).wait_send()
    for copy in across:
        copy.wait_send()

    def row_end(k, _):
        row_push(k).wait_send()
        return 0

    def col_end(k, _):
        col_push(k).wait_send()
        return 0

    lax.fori_loop(1, ROWS, row_end, 0)
    lax.fori_loop(1, COLS, col_end, 0)


def exchange(amp_rows, amp_cols):
    dma = pltpu.SemaphoreType.DMA
    return pl.pallas_call(
        exchange_kernel,
        out_shape=(
            jax.ShapeDtypeStruct((CHIPS_X, CHIPS_Z, 16, 16, 128), jnp.bfloat16),
            jax.ShapeDtypeStruct((ROWS, 8, 32, 128), jnp.bfloat16),
        ),
        in_specs=[VMEM, VMEM],
        out_specs=(VMEM, VMEM),
        scratch_shapes=[
            pltpu.VMEM((ROWS, 16, 128), jnp.bfloat16),
            pltpu.VMEM((256, 128), jnp.float32),
            pltpu.VMEM((256, 128), jnp.float32),
            dma((ROWS,)), dma((ROWS,)), dma((COLS,)), dma((COLS,)),
            dma((15,)), dma((15,)), dma((11,)), dma((11,)), dma((10,)), dma((10,)),
        ],
        compiler_params=pltpu.CompilerParams(
            collective_id=1, has_side_effects=True, vmem_limit_bytes=VMEM_LIMIT
        ),
        name="exchange",
    )(amp_rows, amp_cols)


def product_kernel(left, right, out, wide, rhs):
    @pl.when(pl.program_id(0) == 0)
    def _():
        wide[...] = right[...].reshape(4096, 128).astype(jnp.float32)

        def reorder(c, _):
            for q in range(8):
                rhs[
                    pl.ds(pl.multiple_of((q // 4) * 512 + c * 16, 16), 16), pl.ds((q % 4) * 128, 128)
                ] = wide[pl.ds(q * 32 + c, 16, stride=256), :].astype(jnp.bfloat16)
            return 0

        lax.fori_loop(0, COLS, reorder, 0)

    real = left[:, pl.program_id(0)].reshape(512, 128)
    imag = left[:, 8 + pl.program_id(0)].reshape(512, 128)
    lhs = jnp.concatenate(
        [jnp.concatenate([real, imag], axis=0), jnp.concatenate([imag, -real], axis=0)], axis=1
    )
    got = lax.dot_general(
        lhs, rhs[...], (((0,), (0,)), ((), ())), preferred_element_type=jnp.float32
    ) * (-1.0 / 512)
    out[0] = got[:128]
    out[1] = got[128:]


def product(left, right):
    return pl.pallas_call(
        product_kernel,
        grid=(8,),
        out_shape=jax.ShapeDtypeStruct((2, 1024, 512), jnp.float32),
        in_specs=[VMEM, VMEM],
        out_specs=pl.BlockSpec((2, 128, 512), lambda j: (0, j, 0)),
        scratch_shapes=[pltpu.VMEM((4096, 128), jnp.float32), pltpu.VMEM((1024, 512), jnp.bfloat16)],
        compiler_params=pltpu.CompilerParams(vmem_limit_bytes=VMEM_LIMIT),
        name="product",
    )(left.reshape(COLS, 16, 16, 128), right)


def local(val_waves, cond_waves, val_energy, cond_energy, val_index, cond_index, grid_index):
    pair_start = lax.axis_index("row") * COLS
    val_sel = lax.dynamic_slice_in_dim(val_index, pair_start, COLS)
    cond_sel = lax.dynamic_slice_in_dim(cond_index, pair_start, COLS)
    val_match = val_sel[:, None] == jnp.arange(val_energy.shape[0], dtype=jnp.int32)[None, :]
    cond_match = cond_sel[:, None] == jnp.arange(cond_energy.shape[0], dtype=jnp.int32)[None, :]
    val_level = jnp.sum(jnp.where(val_match, val_energy[None, :], 0.0), axis=1)
    cond_level = jnp.sum(jnp.where(cond_match, cond_energy[None, :], 0.0), axis=1)
    factor = jnp.sqrt(4.0 / (cond_level - val_level)) / GRID**1.5
    waves = jnp.concatenate([val_waves, cond_waves], axis=1).reshape(2, BANDS_DEV, 2, GRID, GRID)
    own = jnp.transpose(waves, (1, 2, 3, 0, 4)).reshape(BANDS_DEV, 128, 128)
    val_slot = jnp.stack([val_sel, val_sel * 0], axis=1)
    cond_slot = jnp.stack([cond_sel // 4, cond_sel % 4 + 1], axis=1)
    dens = pair_densities(val_slot, cond_slot, factor, own)
    amp_rows, amp_cols = spectrum(dens, grid_index)
    left, right = exchange(amp_rows, amp_cols)
    return product(left, right)


def solution(mesh):
    placed = (P(None, "row", "col", None), P(None, "row", "col", None), P(), P(), P(), P(), P())
    return jax.shard_map(
        local, mesh=mesh, in_specs=placed, out_specs=P(None, "row", "col"), check_vma=False
    )
```

```python
import math

import jax
import jax.numpy as jnp
import numpy as np
from jax import lax
from jax.experimental import pallas as pl
from jax.experimental.pallas import tpu as pltpu
from jax.sharding import PartitionSpec as P

GRID = 64
ROWS = 16
COLS = 32
CHIPS_Y = 8
CHIPS_X = 4
CHIPS_Z = 8
BANDS_DEV = 5
VMEM = pl.BlockSpec(memory_space=pltpu.VMEM)
SMEM = pl.BlockSpec(memory_space=pltpu.SMEM)
MESH = pl.DeviceIdType.MESH
VMEM_LIMIT = 56 * 1024 * 1024
CHUNKS = 4
CHUNK = 128 // CHUNKS


def remote(src, dst, send, recv, **where):
    return pltpu.make_async_remote_copy(
        src_ref=src, dst_ref=dst, send_sem=send, recv_sem=recv,
        device_id=where, device_id_type=MESH,
    )


def shifted(value, step, size):
    return lax.rem(value + step + size, size)


class RowGather:
    MATES = {0: 7, -1: 8, -2: 9, 1: 10, 2: 11, -3: 12, -4: 13, 3: 14}

    def __init__(self, view, send, recv):
        r = lax.axis_index("row")
        self.y, self.core = r // 2, r % 2
        self.view, self.send, self.recv = view, send, recv

    def copy(self, number, block, toward):
        ref = self.view(shifted(self.y, block, CHIPS_Y) * 2 + self.core)
        target = shifted(self.y, toward, CHIPS_Y) * 2 + self.core
        return remote(ref, ref, self.send(number), self.recv(number), row=target)

    def mate(self, block):
        ref = self.view(shifted(self.y, block, CHIPS_Y) * 2 + self.core)
        number = self.MATES[block]
        return remote(ref, ref, self.send(number), self.recv(number), row=self.y * 2 + 1 - self.core)

    def hop(self, number):
        block, toward = ((0, 1), (0, 2), (0, -1), (0, -2), (-2, 1), (-2, 2), (2, -1))[number]
        return self.copy(number, block, toward)

    def start(self):
        for number in (0, 2, 1, 3):
            self.hop(number).start()
        self.mate(0).start()

    def middle(self):
        self.hop(1).wait_recv()
        self.hop(4).start()
        self.hop(5).start()
        self.hop(3).wait_recv()
        self.hop(6).start()
        self.hop(0).wait_recv()
        self.hop(2).wait_recv()
        for block in (-1, 1, -2, 2):
            self.mate(block).start()

    def end(self):
        for number, block in ((4, -3), (6, 3), (5, -4)):
            self.hop(number).wait_recv()
            self.mate(block).start()
        for block in self.MATES:
            self.mate(block).wait_recv()

    def finish(self):
        for number in range(7):
            self.hop(number).wait_send()
        for block in self.MATES:
            self.mate(block).wait_send()


class ColGather:
    Z_STEPS = (1, -1, 2, -2, 3, -3, 4)
    X_STEPS = (1, -1, 2)

    def __init__(self, view, send, recv):
        c = lax.axis_index("col")
        self.x, self.z = c // CHIPS_Z, c % CHIPS_Z
        self.view, self.send, self.recv = view, send, recv

    def along_z(self, i):
        ref = self.view(self.x, self.z)
        target = self.x * CHIPS_Z + shifted(self.z, self.Z_STEPS[i], CHIPS_Z)
        return remote(ref, ref, self.send(i), self.recv(i), col=target)

    def along_x(self, i, j):
        block = self.z if i == 0 else shifted(self.z, -self.Z_STEPS[i - 1], CHIPS_Z)
        ref = self.view(self.x, block)
        number = 7 + 3 * i + j
        target = shifted(self.x, self.X_STEPS[j], CHIPS_X) * CHIPS_Z + self.z
        return remote(ref, ref, self.send(number), self.recv(number), col=target)

    def spread(self, i):
        for j in range(3):
            self.along_x(i, j).start()

    def start(self):
        for i in range(7):
            self.along_z(i).start()
        self.spread(0)

    def forward(self, i):
        self.along_z(i).wait_recv()
        self.spread(i + 1)

    def arrive(self):
        for i in range(8):
            for j in range(3):
                self.along_x(i, j).wait_recv()

    def finish(self):
        for i in range(7):
            self.along_z(i).wait_send()
        for i in range(8):
            for j in range(3):
                self.along_x(i, j).wait_send()


def tables():
    angle = 2.0 * math.pi / GRID * (np.outer(np.arange(GRID), np.arange(GRID)) % GRID)
    cos, sin = np.cos(angle), np.sin(angle)

    def split(table):
        high = table.astype(jnp.bfloat16)
        low = (table - high.astype(np.float64)).astype(jnp.bfloat16)
        return high, low

    z_high, z_low = split(np.block([[cos, -sin], [sin, cos]]))
    left_high, left_low = split(np.concatenate([cos, sin], axis=0))
    z_table = np.concatenate([z_high, z_low], axis=0)
    left_table = np.concatenate([left_high, left_low, left_high], axis=1)
    return jnp.asarray(z_table), jnp.asarray(left_table)


def window_kernel(
    val_index, cond_index, val_energy, cond_energy, own, z_table, left_table, index,
    left, rhs,
    bands_0, bands_1, bands_2, bands_3, staged, dens, first, second, picked, amp, row_land, col_land, right, wide,
    band_send, band_recv, pair_send, pair_recv, row_send, row_recv, col_send, col_recv,
    left_send, left_recv, right_send, right_recv,
):
    r, c = lax.axis_index("row"), lax.axis_index("col")
    x, z = c // CHIPS_Z, c % CHIPS_Z
    barrier = pltpu.get_barrier_semaphore()
    for k in range(1, ROWS):
        pl.semaphore_signal(barrier, inc=1, device_id={"row": lax.rem(r + k, ROWS)}, device_id_type=MESH)
    for k in range(1, COLS):
        pl.semaphore_signal(barrier, inc=1, device_id={"col": lax.rem(c + k, COLS)}, device_id_type=MESH)
    bands = (bands_0, bands_1, bands_2, bands_3)
    for q in range(CHUNKS):
        bands[q][r] = own[:, pl.ds(CHUNK * q, CHUNK)]
    pl.semaphore_wait(barrier, ROWS + COLS - 2)

    lane = lax.broadcasted_iota(jnp.int32, (CHUNK, 128), 1)

    def band_part(q):
        return RowGather(
            lambda slot: bands[q].at[slot],
            lambda n: band_send.at[q, n],
            lambda n: band_recv.at[q, n],
        )

    def density(pair, q):
        v, w = val_index[r * COLS + pair], cond_index[r * COLS + pair]
        bra = bands[q][v, 0].astype(jnp.float32)
        ket = bands[q][w // 4, 1 + w % 4].astype(jnp.float32)
        gap = jnp.full((CHUNK, 128), cond_energy[w] - val_energy[v], jnp.float32)
        factor = jnp.sqrt(4.0 / gap) * (1.0 / 512)
        same = bra * ket
        cross = bra * pltpu.roll(ket, 64, 1)
        real = same + pltpu.roll(same, 64, 1)
        imag = pltpu.roll(cross, 64, 1) - cross
        return (jnp.where(lane < 64, real, imag) * factor).astype(jnp.bfloat16)

    def pair_copy(k, q):
        to = lax.rem(c + k, COLS)
        rows = pl.ds(CHUNK * q, CHUNK)
        return remote(
            staged.at[to, rows], dens.at[c, rows], pair_send.at[q, k], pair_recv.at[q, k], col=to
        )

    def pair_part(q):
        def step(k, _):
            to = lax.rem(c + k, COLS)
            staged[to, pl.ds(CHUNK * q, CHUNK)] = density(to, q)
            pair_copy(k, q).start()
            return 0

        lax.fori_loop(1, COLS, step, 0)
        dens[c, pl.ds(CHUNK * q, CHUNK)] = density(c, q)

    parts = [band_part(q) for q in range(CHUNKS)]
    parts[0].start()
    if CHUNKS > 1:
        parts[1].start()
    parts[0].middle()
    for q in range(CHUNKS):
        if q + 2 < CHUNKS:
            parts[q + 2].start()
        if q + 1 < CHUNKS:
            parts[q + 1].middle()
        parts[q].end()
        pair_part(q)

    z_tab = z_table[...]
    left_tab = left_table[...]
    sign = jnp.where(lax.broadcasted_iota(jnp.int32, (64, 128), 1) < 64, 1.0, -1.0)

    def transform(parts):
        high = [p.astype(jnp.bfloat16) for p in parts]
        low = [(p - h.astype(jnp.float32)).astype(jnp.bfloat16) for p, h in zip(parts, high)]
        high = jnp.concatenate(high, axis=1)
        low = jnp.concatenate(low, axis=1)
        got = jnp.dot(
            left_tab, jnp.concatenate([high, high, low], axis=0), preferred_element_type=jnp.float32
        )
        return [
            got[:64, 128 * n : 128 * (n + 1)]
            + sign * pltpu.roll(got[64:, 128 * n : 128 * (n + 1)], 64, 1)
            for n in range(len(parts))
        ]

    for q in range(CHUNKS):
        def arrived(k, _):
            origin = lax.rem(c - k + COLS, COLS)
            rows = pl.ds(CHUNK * q, CHUNK)
            remote(
                staged.at[origin, rows], dens.at[origin, rows], pair_send.at[q, k], pair_recv.at[q, k],
                col=origin,
            ).wait_recv()
            return 0

        lax.fori_loop(1, COLS, arrived, 0)
        part = dens[:, pl.ds(CHUNK * q, CHUNK)].reshape(COLS * CHUNK, 128)
        got = jnp.dot(
            jnp.concatenate([part, part], axis=1), z_tab, preferred_element_type=jnp.float32
        )
        first[:, pl.ds(CHUNK * q, CHUNK)] = got.reshape(COLS, CHUNK, 128)
        if (q + 1) * CHUNK % 64 == 0:
            plane = (q + 1) * CHUNK // 64 - 1

            def along_y(i, _):
                got = transform([first[i * 8 + n, pl.ds(64 * plane, 64)] for n in range(8)])
                for n in range(8):
                    base = pl.multiple_of((i * 8 + n) * 128 + 64 * plane, 64)
                    second[pl.ds(base, 64), :] = got[n]
                return 0

            lax.fori_loop(0, 4, along_y, 0)

    for i in range(8):
        done = transform([second[pl.ds(i * 8 + n, 64, stride=64), :] for n in range(8)])
        for n in range(4):
            tile = jnp.concatenate(done[2 * n : 2 * n + 2], axis=0)
            number = i * 4 + n
            picked[
                pl.ds((number // 8) * 128, 128), pl.ds((number % 8) * 128, 128)
            ] = tile.T.astype(jnp.bfloat16)

    inner = lax.broadcasted_iota(jnp.int32, (1024, 1024), 0)
    outer = lax.broadcasted_iota(jnp.int32, (256, 1024), 0)

    def row_copy(b, h, rr):
        return remote(amp.at[b], row_land.at[h, r], row_send.at[b], row_recv.at[h, r], row=rr)

    def col_copy(b):
        return remote(amp.at[b], col_land.at[c], col_send.at[b], col_recv.at[c], col=b)

    def select(h):
        def step(t, _):
            blocks = (4 * t + h, 4 * t + 2 + h)
            spot = jnp.concatenate(
                [index[pl.ds(4 * b + i, 1), :] for b in blocks for i in range(4)], axis=1
            )
            kx, ky, kz = spot // 4096, (spot // 64) % 64, spot % 64
            hot = jnp.where(inner == (ky % 16) * 64 + kx, 1.0, 0.0).astype(jnp.bfloat16)
            got = jnp.dot(picked[...], hot, preferred_element_type=jnp.float32)
            keep = outer == (ky // 16) * 64 + kz
            for part in range(2):
                half = jnp.concatenate(
                    [got[128 * g + 64 * part : 128 * g + 64 * part + 64] for g in range(4)], axis=0
                )
                row = jnp.sum(jnp.where(keep, half, 0.0), axis=0, keepdims=True)
                for j in range(8):
                    amp[blocks[j // 4], pl.ds(4 * part + j % 4, 1), :] = row[:, 128 * j : 128 * (j + 1)]
            for n, b in enumerate(blocks):
                rr = 2 * t + n

                @pl.when(rr != r)
                def _():
                    row_copy(b, h, rr).start()

                @pl.when(rr == r)
                def _():
                    row_land[h, r] = amp[b]

                @pl.when(b != c)
                def _():
                    col_copy(b).start()

                @pl.when(b == c)
                def _():
                    col_land[c] = amp[b]
            return 0

        return step

    def row_half(h):
        def settle(k, _):
            origin = lax.rem(r - k + ROWS, ROWS)
            remote(
                amp.at[0], row_land.at[h, origin], row_send.at[0], row_recv.at[h, origin], row=origin
            ).wait_recv()
            return 0

        lax.fori_loop(1, ROWS, settle, 0)
        wide[pl.ds(0, 128), :] = row_land[h].reshape(128, 128)
        for j in range(8):
            left[h, x, z, j] = wide[pl.ds(j, 16, stride=8), :].astype(jnp.bfloat16)
        return ColGather(
            lambda xx, zz: left.at[h, xx, zz], lambda n: left_send.at[h, n], lambda n: left_recv.at[h, n]
        )

    lax.fori_loop(0, 8, select(0), 0)
    early = row_half(0)
    early.start()
    for low, high, ready in ((0, 2, (0, 1)), (2, 4, (2, 3)), (4, 6, (4, 5, 6)), (6, 8, ())):
        lax.fori_loop(low, high, select(1), 0)
        for i in ready:
            early.forward(i)
    late = row_half(1)
    late.start()

    def col_settle(k, _):
        origin = lax.rem(c - k + COLS, COLS)
        remote(
            amp.at[0], col_land.at[origin], col_send.at[0], col_recv.at[origin], col=origin
        ).wait_recv()
        return 0

    lax.fori_loop(1, COLS, col_settle, 0)
    wide[pl.ds(0, 256), :] = col_land[...].reshape(256, 128)
    for j in range(8):
        right[r, j] = wide[pl.ds(j, 32, stride=8), :].astype(jnp.bfloat16)
    column = RowGather(lambda slot: right.at[slot], lambda n: right_send.at[n], lambda n: right_recv.at[n])
    column.start()
    for i in range(4):
        late.forward(i)
    column.middle()
    for i in range(4, 7):
        late.forward(i)
    column.end()

    wide[...] = right[...].reshape(4096, 128).astype(jnp.float32)

    def reorder(n, _):
        for q in range(8):
            rhs[
                pl.ds(pl.multiple_of((q // 4) * 512 + n * 16, 16), 16), pl.ds((q % 4) * 128, 128)
            ] = wide[pl.ds(q * 32 + n, 16, stride=256), :].astype(jnp.bfloat16)
        return 0

    lax.fori_loop(0, COLS, reorder, 0)

    for part in parts:
        part.finish()

    def pair_end(k, _):
        for q in range(CHUNKS):
            pair_copy(k, q).wait_send()
        return 0

    lax.fori_loop(1, COLS, pair_end, 0)

    def amp_end(b, _):
        @pl.when(b // 2 != r)
        def _():
            row_copy(b, b % 2, b // 2).wait_send()

        @pl.when(b != c)
        def _():
            col_copy(b).wait_send()

        return 0

    lax.fori_loop(0, COLS, amp_end, 0)
    early.arrive()
    late.arrive()
    early.finish()
    late.finish()
    column.finish()


def window(val_index, cond_index, val_energy, cond_energy, own, index):
    z_table, left_table = tables()
    dma = pltpu.SemaphoreType.DMA
    f32, bf16 = jnp.float32, jnp.bfloat16
    return pl.pallas_call(
        window_kernel,
        out_shape=(
            jax.ShapeDtypeStruct((2, CHIPS_X, CHIPS_Z, 8, 16, 128), bf16),
            jax.ShapeDtypeStruct((1024, 512), bf16),
        ),
        in_specs=[SMEM] * 4 + [VMEM] * 4,
        out_specs=(VMEM, VMEM),
        scratch_shapes=[
            *[pltpu.VMEM((ROWS, BANDS_DEV, CHUNK, 128), bf16) for _ in range(CHUNKS)],
            pltpu.VMEM((COLS, 128, 128), bf16),
            pltpu.VMEM((COLS, 128, 128), bf16),
            pltpu.VMEM((COLS, 128, 128), f32),
            pltpu.VMEM((4096, 128), f32),
            pltpu.VMEM((512, 1024), bf16),
            pltpu.VMEM((COLS, 8, 128), f32),
            pltpu.VMEM((2, ROWS, 8, 128), f32),
            pltpu.VMEM((COLS, 8, 128), f32),
            pltpu.VMEM((ROWS, 8, COLS, 128), bf16),
            pltpu.VMEM((4096, 128), f32),
            dma((CHUNKS, 15)), dma((CHUNKS, 15)), dma((CHUNKS, COLS)), dma((CHUNKS, COLS)),
            dma((COLS,)), dma((2, ROWS)), dma((COLS,)), dma((COLS,)),
            dma((2, 31)), dma((2, 31)), dma((15,)), dma((15,)),
        ],
        compiler_params=pltpu.CompilerParams(
            collective_id=0, has_side_effects=True, vmem_limit_bytes=VMEM_LIMIT
        ),
        name="window",
    )(val_index, cond_index, val_energy, cond_energy, own, z_table, left_table, index)


def product_kernel(real, imag, rhs, out):
    real = real[...].reshape(512, 128)
    imag = imag[...].reshape(512, 128)
    lhs = jnp.concatenate(
        [jnp.concatenate([real, imag], axis=0), jnp.concatenate([imag, -real], axis=0)], axis=1
    )
    got = lax.dot_general(
        lhs, rhs[...], (((0,), (0,)), ((), ())), preferred_element_type=jnp.float32
    ) * (-1.0 / 512)
    out[0] = got[:128]
    out[1] = got[128:]


def product(left, rhs):
    block = (1, CHIPS_X, CHIPS_Z, 1, 16, 128)
    return pl.pallas_call(
        product_kernel,
        grid=(8,),
        out_shape=jax.ShapeDtypeStruct((2, 1024, 512), jnp.float32),
        in_specs=[
            pl.BlockSpec(block, lambda j: (j // 4, 0, 0, j % 4, 0, 0)),
            pl.BlockSpec(block, lambda j: (j // 4, 0, 0, j % 4 + 4, 0, 0)),
            VMEM,
        ],
        out_specs=pl.BlockSpec((2, 128, 512), lambda j: (0, j, 0)),
        compiler_params=pltpu.CompilerParams(vmem_limit_bytes=VMEM_LIMIT),
        name="product",
    )(left, left, rhs)


def local(val_waves, cond_waves, val_energy, cond_energy, val_index, cond_index, grid_index):
    waves = jnp.concatenate([val_waves, cond_waves], axis=1).reshape(2, BANDS_DEV, 2, GRID, GRID)
    own = jnp.transpose(waves, (1, 2, 3, 0, 4)).reshape(BANDS_DEV, 128, 128)
    left, rhs = window(
        val_index, cond_index, val_energy, cond_energy, own, grid_index.reshape(128, 128)
    )
    return product(left, rhs)


def solution(mesh):
    placed = (P(None, "row", "col", None), P(None, "row", "col", None), P(), P(), P(), P(), P())
    return jax.shard_map(
        local, mesh=mesh, in_specs=placed, out_specs=P(None, "row", "col"), check_vma=False
    )
```

```python
import math

import jax
import jax.numpy as jnp
import numpy as np
from jax import lax
from jax.experimental import pallas as pl
from jax.experimental.pallas import tpu as pltpu
from jax.sharding import PartitionSpec as P

GRID = 64
ROWS = 16
COLS = 32
CHIPS_Y = 8
CHIPS_X = 4
CHIPS_Z = 8
BANDS_DEV = 5
VMEM = pl.BlockSpec(memory_space=pltpu.VMEM)
SMEM = pl.BlockSpec(memory_space=pltpu.SMEM)
MESH = pl.DeviceIdType.MESH
VMEM_LIMIT = 56 * 1024 * 1024
SLAB = 16
GROUP = 8
Y_STEPS = (1, -1, 2, -2, 3, -3, 4)


def remote(src, dst, send, recv, **where):
    return pltpu.make_async_remote_copy(
        src_ref=src, dst_ref=dst, send_sem=send, recv_sem=recv,
        device_id=where, device_id_type=MESH,
    )


def shifted(value, step, size):
    return lax.rem(value + step + size, size)


class RowGather:
    MATES = {0: 7, -1: 8, -2: 9, 1: 10, 2: 11, -3: 12, -4: 13, 3: 14}

    def __init__(self, view, send, recv):
        r = lax.axis_index("row")
        self.y, self.core = r // 2, r % 2
        self.view, self.send, self.recv = view, send, recv

    def copy(self, number, block, toward):
        ref = self.view(shifted(self.y, block, CHIPS_Y) * 2 + self.core)
        target = shifted(self.y, toward, CHIPS_Y) * 2 + self.core
        return remote(ref, ref, self.send(number), self.recv(number), row=target)

    def mate(self, block):
        ref = self.view(shifted(self.y, block, CHIPS_Y) * 2 + self.core)
        number = self.MATES[block]
        return remote(ref, ref, self.send(number), self.recv(number), row=self.y * 2 + 1 - self.core)

    def hop(self, number):
        block, toward = ((0, 1), (0, 2), (0, -1), (0, -2), (-2, 1), (-2, 2), (2, -1))[number]
        return self.copy(number, block, toward)

    def start(self):
        for number in (0, 2, 1, 3):
            self.hop(number).start()
        self.mate(0).start()

    def middle(self):
        self.hop(1).wait_recv()
        self.hop(4).start()
        self.hop(5).start()
        self.hop(3).wait_recv()
        self.hop(6).start()
        self.hop(0).wait_recv()
        self.hop(2).wait_recv()
        for block in (-1, 1, -2, 2):
            self.mate(block).start()

    def end(self):
        for number, block in ((4, -3), (6, 3), (5, -4)):
            self.hop(number).wait_recv()
            self.mate(block).start()
        for block in self.MATES:
            self.mate(block).wait_recv()

    def finish(self):
        for number in range(7):
            self.hop(number).wait_send()
        for block in self.MATES:
            self.mate(block).wait_send()


class ColGather:
    Z_STEPS = (1, -1, 2, -2, 3, -3, 4)
    X_STEPS = (1, -1, 2)

    def __init__(self, view, send, recv):
        c = lax.axis_index("col")
        self.x, self.z = c // CHIPS_Z, c % CHIPS_Z
        self.view, self.send, self.recv = view, send, recv

    def along_z(self, i):
        ref = self.view(self.x, self.z)
        target = self.x * CHIPS_Z + shifted(self.z, self.Z_STEPS[i], CHIPS_Z)
        return remote(ref, ref, self.send(i), self.recv(i), col=target)

    def along_x(self, i, j):
        block = self.z if i == 0 else shifted(self.z, -self.Z_STEPS[i - 1], CHIPS_Z)
        ref = self.view(self.x, block)
        number = 7 + 3 * i + j
        target = shifted(self.x, self.X_STEPS[j], CHIPS_X) * CHIPS_Z + self.z
        return remote(ref, ref, self.send(number), self.recv(number), col=target)

    def spread(self, i):
        for j in range(3):
            self.along_x(i, j).start()

    def start(self):
        for i in range(7):
            self.along_z(i).start()
        self.spread(0)

    def forward(self, i):
        self.along_z(i).wait_recv()
        self.spread(i + 1)

    def arrive(self):
        for i in range(8):
            for j in range(3):
                self.along_x(i, j).wait_recv()

    def finish(self):
        for i in range(7):
            self.along_z(i).wait_send()
        for i in range(8):
            for j in range(3):
                self.along_x(i, j).wait_send()


def tables():
    angle = 2.0 * math.pi / GRID * (np.outer(np.arange(GRID), np.arange(GRID)) % GRID)
    cos, sin = np.cos(angle), np.sin(angle)

    def split(table):
        high = table.astype(jnp.bfloat16)
        low = (table - high.astype(np.float64)).astype(jnp.bfloat16)
        return high, low

    z_high, z_low = split(np.block([[cos, -sin], [sin, cos]]))
    left_high, left_low = split(np.concatenate([cos, sin], axis=0))
    z_table = np.concatenate([z_high, z_low], axis=0)
    left_table = np.concatenate([left_high, left_low, left_high], axis=1)
    return jnp.asarray(z_table), jnp.asarray(left_table)


def window_kernel(
    val_index, cond_index, val_energy, cond_energy, own, z_table, left_table, index,
    left, rhs,
    bands, staged, dens, first, second, picked, amp, row_land, col_land, right, wide,
    band_send, band_recv, pair_send, pair_recv, row_send, row_recv, col_send, col_recv,
    left_send, left_recv, right_send, right_recv,
):
    r, c = lax.axis_index("row"), lax.axis_index("col")
    x, z = c // CHIPS_Z, c % CHIPS_Z
    y, core = r // 2, r % 2
    def slab(chip):
        return pl.ds(pl.multiple_of(chip * SLAB, SLAB), SLAB)

    barrier = pltpu.get_barrier_semaphore()
    for k in range(1, ROWS):
        pl.semaphore_signal(barrier, inc=1, device_id={"row": lax.rem(r + k, ROWS)}, device_id_type=MESH)
    for k in range(1, COLS):
        pl.semaphore_signal(barrier, inc=1, device_id={"col": lax.rem(c + k, COLS)}, device_id_type=MESH)
    bands[r] = own[:, slab(y)]
    pl.semaphore_wait(barrier, ROWS + COLS - 2)

    def band_push(i):
        chip = shifted(y, Y_STEPS[i], CHIPS_Y)
        return remote(
            own.at[:, slab(chip)], bands.at[r], band_send.at[i], band_recv.at[i], row=chip * 2 + core
        )

    def band_mate(i):
        ref = bands.at[r if i == 7 else shifted(y, -Y_STEPS[i], CHIPS_Y) * 2 + core]
        return remote(ref, ref, band_send.at[8 + i], band_recv.at[8 + i], row=y * 2 + 1 - core)

    for i in range(7):
        band_push(i).start()
    band_mate(7).start()
    for i in range(7):
        band_push(i).wait_recv()
        band_mate(i).start()
    for i in range(8):
        band_mate(i).wait_recv()

    lane = lax.broadcasted_iota(jnp.int32, (SLAB, 128), 1)

    def density(pair):
        v, w = val_index[pair], cond_index[pair]
        bra = bands[v, 0].astype(jnp.float32)
        ket = bands[w // 4, 1 + w % 4].astype(jnp.float32)
        gap = jnp.full((8, 128), cond_energy[w] - val_energy[v], jnp.float32)
        factor = jnp.sqrt(4.0 / gap) * (1.0 / 512)
        factor = jnp.concatenate([factor, factor], axis=0)
        same = bra * ket
        cross = bra * pltpu.roll(ket, 64, 1)
        real = same + pltpu.roll(same, 64, 1)
        imag = pltpu.roll(cross, 64, 1) - cross
        return (jnp.where(lane < 64, real, imag) * factor).astype(jnp.bfloat16)

    def produce(n, _):
        turn, first_col = lax.rem(n * 3, CHIPS_Y), (n // CHIPS_Y) * GROUP
        row = shifted(y, turn, CHIPS_Y) * 2 + core
        cols = [lax.rem(c + first_col + i, COLS) for i in range(GROUP)]
        for to in cols:
            staged[turn, to] = density(row * COLS + to)
        for i, to in enumerate(cols):
            copy = remote(
                staged.at[turn, to], dens.at[c, slab(y)], pair_send.at[turn], pair_recv.at[turn],
                row=row, col=to,
            )
            if i > 0:
                copy.start()
            else:
                @pl.when(n > 0)
                def _():
                    copy.start()

                @pl.when(n == 0)
                def _():
                    dens[c, slab(y)] = staged[0, c]
        return 0

    lax.fori_loop(0, CHIPS_Y * COLS // GROUP, produce, 0)

    def pair_group(turn):
        count = COLS - 1 if isinstance(turn, int) else COLS
        return remote(
            staged.at[turn, pl.ds(0, count)],
            dens.at[pl.ds(0, count), slab(shifted(y, -turn, CHIPS_Y))],
            pair_send.at[turn], pair_recv.at[turn],
            row=shifted(y, 1, CHIPS_Y) * 2 + core, col=c,
        )

    z_tab = z_table[...]
    left_tab = left_table[...]
    sign = jnp.where(lax.broadcasted_iota(jnp.int32, (64, 128), 1) < 64, 1.0, -1.0)

    def transform(parts):
        high = [p.astype(jnp.bfloat16) for p in parts]
        low = [(p - h.astype(jnp.float32)).astype(jnp.bfloat16) for p, h in zip(parts, high)]
        high = jnp.concatenate(high, axis=1)
        low = jnp.concatenate(low, axis=1)
        got = jnp.dot(
            left_tab, jnp.concatenate([high, high, low], axis=0), preferred_element_type=jnp.float32
        )
        return [
            got[:64, 128 * n : 128 * (n + 1)]
            + sign * pltpu.roll(got[64:, 128 * n : 128 * (n + 1)], 64, 1)
            for n in range(len(parts))
        ]

    def along_z(chip):
        part = dens[:, slab(chip)].reshape(COLS * SLAB, 128)
        got = jnp.dot(
            jnp.concatenate([part, part], axis=1), z_tab, preferred_element_type=jnp.float32
        )
        first[:, slab(chip)] = got.reshape(COLS, SLAB, 128)

    def arrived(turn, _):
        pair_group(turn).wait_recv()
        along_z(shifted(y, -turn, CHIPS_Y))
        return 0

    pair_group(0).wait_recv()
    along_z(y)
    lax.fori_loop(1, CHIPS_Y, arrived, 0)

    for plane in range(2):
        def along_y(i, _):
            got = transform([first[i * 8 + n, pl.ds(64 * plane, 64)] for n in range(8)])
            for n in range(8):
                base = pl.multiple_of((i * 8 + n) * 128 + 64 * plane, 64)
                second[pl.ds(base, 64), :] = got[n]
            return 0

        lax.fori_loop(0, 4, along_y, 0)

    for i in range(8):
        done = transform([second[pl.ds(i * 8 + n, 64, stride=64), :] for n in range(8)])
        for n in range(4):
            tile = jnp.concatenate(done[2 * n : 2 * n + 2], axis=0)
            number = i * 4 + n
            picked[
                pl.ds((number // 8) * 128, 128), pl.ds((number % 8) * 128, 128)
            ] = tile.T.astype(jnp.bfloat16)

    inner = lax.broadcasted_iota(jnp.int32, (1024, 1024), 0)
    outer = lax.broadcasted_iota(jnp.int32, (256, 1024), 0)

    def row_copy(b, h, rr):
        return remote(amp.at[b], row_land.at[h, r], row_send.at[b], row_recv.at[h, r], row=rr)

    def col_copy(b):
        return remote(amp.at[b], col_land.at[c], col_send.at[b], col_recv.at[c], col=b)

    def select(h):
        def step(t, _):
            blocks = (4 * t + h, 4 * t + 2 + h)
            spot = jnp.concatenate(
                [index[pl.ds(4 * b + i, 1), :] for b in blocks for i in range(4)], axis=1
            )
            kx, ky, kz = spot // 4096, (spot // 64) % 64, spot % 64
            hot = jnp.where(inner == (ky % 16) * 64 + kx, 1.0, 0.0).astype(jnp.bfloat16)
            got = jnp.dot(picked[...], hot, preferred_element_type=jnp.float32)
            keep = outer == (ky // 16) * 64 + kz
            for part in range(2):
                half = jnp.concatenate(
                    [got[128 * g + 64 * part : 128 * g + 64 * part + 64] for g in range(4)], axis=0
                )
                row = jnp.sum(jnp.where(keep, half, 0.0), axis=0, keepdims=True)
                for j in range(8):
                    amp[blocks[j // 4], pl.ds(4 * part + j % 4, 1), :] = row[:, 128 * j : 128 * (j + 1)]
            for n, b in enumerate(blocks):
                rr = 2 * t + n

                @pl.when(rr != r)
                def _():
                    row_copy(b, h, rr).start()

                @pl.when(rr == r)
                def _():
                    row_land[h, r] = amp[b]

                @pl.when(b != c)
                def _():
                    col_copy(b).start()

                @pl.when(b == c)
                def _():
                    col_land[c] = amp[b]
            return 0

        return step

    def row_half(h):
        def settle(k, _):
            origin = lax.rem(r - k + ROWS, ROWS)
            remote(
                amp.at[0], row_land.at[h, origin], row_send.at[0], row_recv.at[h, origin], row=origin
            ).wait_recv()
            return 0

        lax.fori_loop(1, ROWS, settle, 0)
        wide[pl.ds(0, 128), :] = row_land[h].reshape(128, 128)
        for j in range(8):
            left[h, x, z, j] = wide[pl.ds(j, 16, stride=8), :].astype(jnp.bfloat16)
        return ColGather(
            lambda xx, zz: left.at[h, xx, zz], lambda n: left_send.at[h, n], lambda n: left_recv.at[h, n]
        )

    lax.fori_loop(0, 8, select(0), 0)
    early = row_half(0)
    early.start()
    for low, high, ready in ((0, 2, (0, 1)), (2, 4, (2, 3)), (4, 6, (4, 5, 6)), (6, 8, ())):
        lax.fori_loop(low, high, select(1), 0)
        for i in ready:
            early.forward(i)
    late = row_half(1)
    late.start()

    def col_settle(k, _):
        origin = lax.rem(c - k + COLS, COLS)
        remote(
            amp.at[0], col_land.at[origin], col_send.at[0], col_recv.at[origin], col=origin
        ).wait_recv()
        return 0

    lax.fori_loop(1, COLS, col_settle, 0)
    wide[pl.ds(0, 256), :] = col_land[...].reshape(256, 128)
    for j in range(8):
        right[r, j] = wide[pl.ds(j, 32, stride=8), :].astype(jnp.bfloat16)
    column = RowGather(lambda slot: right.at[slot], lambda n: right_send.at[n], lambda n: right_recv.at[n])
    column.start()
    for i in range(4):
        late.forward(i)
    column.middle()
    for i in range(4, 7):
        late.forward(i)
    column.end()

    wide[...] = right[...].reshape(4096, 128).astype(jnp.float32)

    def reorder(n, _):
        for q in range(8):
            rhs[
                pl.ds(pl.multiple_of((q // 4) * 512 + n * 16, 16), 16), pl.ds((q % 4) * 128, 128)
            ] = wide[pl.ds(q * 32 + n, 16, stride=256), :].astype(jnp.bfloat16)
        return 0

    lax.fori_loop(0, COLS, reorder, 0)

    for i in range(7):
        band_push(i).wait_send()
    for i in range(8):
        band_mate(i).wait_send()

    def pair_end(turn, _):
        pair_group(turn).wait_send()
        return 0

    pair_group(0).wait_send()
    lax.fori_loop(1, CHIPS_Y, pair_end, 0)

    def amp_end(b, _):
        @pl.when(b // 2 != r)
        def _():
            row_copy(b, b % 2, b // 2).wait_send()

        @pl.when(b != c)
        def _():
            col_copy(b).wait_send()

        return 0

    lax.fori_loop(0, COLS, amp_end, 0)
    early.arrive()
    late.arrive()
    early.finish()
    late.finish()
    column.finish()


def window(val_index, cond_index, val_energy, cond_energy, own, index):
    z_table, left_table = tables()
    dma = pltpu.SemaphoreType.DMA
    f32, bf16 = jnp.float32, jnp.bfloat16
    return pl.pallas_call(
        window_kernel,
        out_shape=(
            jax.ShapeDtypeStruct((2, CHIPS_X, CHIPS_Z, 8, 16, 128), bf16),
            jax.ShapeDtypeStruct((1024, 512), bf16),
        ),
        in_specs=[SMEM] * 4 + [VMEM] * 4,
        out_specs=(VMEM, VMEM),
        scratch_shapes=[
            pltpu.VMEM((ROWS, BANDS_DEV, SLAB, 128), bf16),
            pltpu.VMEM((CHIPS_Y, COLS, SLAB, 128), bf16),
            pltpu.VMEM((COLS, 128, 128), bf16),
            pltpu.VMEM((COLS, 128, 128), f32),
            pltpu.VMEM((4096, 128), f32),
            pltpu.VMEM((512, 1024), bf16),
            pltpu.VMEM((COLS, 8, 128), f32),
            pltpu.VMEM((2, ROWS, 8, 128), f32),
            pltpu.VMEM((COLS, 8, 128), f32),
            pltpu.VMEM((ROWS, 8, COLS, 128), bf16),
            pltpu.VMEM((4096, 128), f32),
            dma((16,)), dma((16,)), dma((CHIPS_Y,)), dma((CHIPS_Y,)),
            dma((COLS,)), dma((2, ROWS)), dma((COLS,)), dma((COLS,)),
            dma((2, 31)), dma((2, 31)), dma((15,)), dma((15,)),
        ],
        compiler_params=pltpu.CompilerParams(
            collective_id=0, has_side_effects=True, vmem_limit_bytes=VMEM_LIMIT
        ),
        name="window",
    )(val_index, cond_index, val_energy, cond_energy, own, z_table, left_table, index)


def product_kernel(left, rhs, out):
    j = pl.program_id(0)
    real = left[j // 4, :, :, j % 4].reshape(512, 128).astype(jnp.float32).T.astype(jnp.bfloat16)
    imag = left[j // 4, :, :, j % 4 + 4].reshape(512, 128).astype(jnp.float32).T.astype(jnp.bfloat16)
    lhs = jnp.concatenate(
        [jnp.concatenate([real, imag], axis=1), jnp.concatenate([imag, -real], axis=1)], axis=0
    )
    got = jnp.dot(lhs, rhs[...], preferred_element_type=jnp.float32) * (-1.0 / 512)
    out[0] = got[:128]
    out[1] = got[128:]


def product(left, rhs):
    block = (1, CHIPS_X, CHIPS_Z, 1, 16, 128)
    return pl.pallas_call(
        product_kernel,
        grid=(8,),
        out_shape=jax.ShapeDtypeStruct((2, 1024, 512), jnp.float32),
        in_specs=[
            VMEM, VMEM,
        ],
        out_specs=pl.BlockSpec((2, 128, 512), lambda j: (0, j, 0)),
        compiler_params=pltpu.CompilerParams(vmem_limit_bytes=VMEM_LIMIT),
        name="product",
    )(left, rhs)


def local(val_waves, cond_waves, val_energy, cond_energy, val_index, cond_index, grid_index):
    waves = jnp.concatenate([val_waves, cond_waves], axis=1).reshape(2, BANDS_DEV, 2, GRID, GRID)
    own = jnp.transpose(waves, (1, 2, 3, 0, 4)).reshape(BANDS_DEV, 128, 128)
    left, rhs = window(
        val_index, cond_index, val_energy, cond_energy, own, grid_index.reshape(128, 128)
    )
    return product(left, rhs)


def solution(mesh):
    placed = (P(None, "row", "col", None), P(None, "row", "col", None), P(), P(), P(), P(), P())
    return jax.shard_map(
        local, mesh=mesh, in_specs=placed, out_specs=P(None, "row", "col"), check_vma=False
    )
```

```python
import math

import jax
import jax.numpy as jnp
import numpy as np
from jax import lax
from jax.experimental import pallas as pl
from jax.experimental.pallas import tpu as pltpu
from jax.sharding import PartitionSpec as P

GRID = 64
ROWS = 16
COLS = 32
CHIPS_Y = 8
CHIPS_X = 4
CHIPS_Z = 8
BANDS_DEV = 5
VMEM = pl.BlockSpec(memory_space=pltpu.VMEM)
SMEM = pl.BlockSpec(memory_space=pltpu.SMEM)
MESH = pl.DeviceIdType.MESH
VMEM_LIMIT = 56 * 1024 * 1024
SLAB = 16
GROUP = 8
Y_STEPS = (1, -1, 2, -2, 3, -3, 4)


def remote(src, dst, send, recv, **where):
    return pltpu.make_async_remote_copy(
        src_ref=src, dst_ref=dst, send_sem=send, recv_sem=recv,
        device_id=where, device_id_type=MESH,
    )


def shifted(value, step, size):
    return lax.rem(value + step + size, size)


class RowGather:
    MATES = {0: 7, -1: 8, -2: 9, 1: 10, 2: 11, -3: 12, -4: 13, 3: 14}

    def __init__(self, view, send, recv):
        r = lax.axis_index("row")
        self.y, self.core = r // 2, r % 2
        self.view, self.send, self.recv = view, send, recv

    def copy(self, number, block, toward):
        ref = self.view(shifted(self.y, block, CHIPS_Y) * 2 + self.core)
        target = shifted(self.y, toward, CHIPS_Y) * 2 + self.core
        return remote(ref, ref, self.send(number), self.recv(number), row=target)

    def mate(self, block):
        ref = self.view(shifted(self.y, block, CHIPS_Y) * 2 + self.core)
        number = self.MATES[block]
        return remote(ref, ref, self.send(number), self.recv(number), row=self.y * 2 + 1 - self.core)

    def hop(self, number):
        block, toward = ((0, 1), (0, 2), (0, -1), (0, -2), (-2, 1), (-2, 2), (2, -1))[number]
        return self.copy(number, block, toward)

    def start(self):
        for number in (0, 2, 1, 3):
            self.hop(number).start()
        self.mate(0).start()

    def middle(self):
        self.hop(1).wait_recv()
        self.hop(4).start()
        self.hop(5).start()
        self.hop(3).wait_recv()
        self.hop(6).start()
        self.hop(0).wait_recv()
        self.hop(2).wait_recv()
        for block in (-1, 1, -2, 2):
            self.mate(block).start()

    def end(self):
        for number, block in ((4, -3), (6, 3), (5, -4)):
            self.hop(number).wait_recv()
            self.mate(block).start()
        for block in self.MATES:
            self.mate(block).wait_recv()

    def finish(self):
        for number in range(7):
            self.hop(number).wait_send()
        for block in self.MATES:
            self.mate(block).wait_send()


class ColGather:
    Z_STEPS = (1, -1, 2, -2, 3, -3, 4)
    X_STEPS = (1, -1, 2)

    def __init__(self, view, send, recv):
        c = lax.axis_index("col")
        self.x, self.z = c // CHIPS_Z, c % CHIPS_Z
        self.view, self.send, self.recv = view, send, recv

    def along_z(self, i):
        ref = self.view(self.x, self.z)
        target = self.x * CHIPS_Z + shifted(self.z, self.Z_STEPS[i], CHIPS_Z)
        return remote(ref, ref, self.send(i), self.recv(i), col=target)

    def along_x(self, i, j):
        block = self.z if i == 0 else shifted(self.z, -self.Z_STEPS[i - 1], CHIPS_Z)
        ref = self.view(self.x, block)
        number = 7 + 3 * i + j
        target = shifted(self.x, self.X_STEPS[j], CHIPS_X) * CHIPS_Z + self.z
        return remote(ref, ref, self.send(number), self.recv(number), col=target)

    def spread(self, i):
        for j in range(3):
            self.along_x(i, j).start()

    def start(self):
        for i in range(7):
            self.along_z(i).start()
        self.spread(0)

    def forward(self, i):
        self.along_z(i).wait_recv()
        self.spread(i + 1)

    def arrive(self):
        for i in range(8):
            for j in range(3):
                self.along_x(i, j).wait_recv()

    def finish(self):
        for i in range(7):
            self.along_z(i).wait_send()
        for i in range(8):
            for j in range(3):
                self.along_x(i, j).wait_send()


def tables():
    angle = 2.0 * math.pi / GRID * (np.outer(np.arange(GRID), np.arange(GRID)) % GRID)
    cos, sin = np.cos(angle), np.sin(angle)

    def split(table):
        high = table.astype(jnp.bfloat16)
        low = (table - high.astype(np.float64)).astype(jnp.bfloat16)
        return high, low

    z_high, z_low = split(np.block([[cos, -sin], [sin, cos]]))
    left_high, left_low = split(np.concatenate([cos, sin], axis=0))
    z_table = np.concatenate([z_high, z_low], axis=0)
    left_table = np.concatenate([left_high, left_low, left_high], axis=1)
    return jnp.asarray(z_table), jnp.asarray(left_table)


def window_kernel(
    val_index, cond_index, val_energy, cond_energy, own, z_table, left_table, index,
    left, rhs,
    bands, staged, dens, first, second, picked, amp, row_land, col_land, right, wide,
    band_send, band_recv, pair_send, pair_recv, row_send, row_recv, col_send, col_recv,
    left_send, left_recv, right_send, right_recv,
):
    r, c = lax.axis_index("row"), lax.axis_index("col")
    x, z = c // CHIPS_Z, c % CHIPS_Z
    y, core = r // 2, r % 2
    def slab(chip):
        return pl.ds(pl.multiple_of(chip * SLAB, SLAB), SLAB)

    barrier = pltpu.get_barrier_semaphore()
    for k in range(1, ROWS):
        pl.semaphore_signal(barrier, inc=1, device_id={"row": lax.rem(r + k, ROWS)}, device_id_type=MESH)
    for k in range(1, COLS):
        pl.semaphore_signal(barrier, inc=1, device_id={"col": lax.rem(c + k, COLS)}, device_id_type=MESH)
    bands[r] = own[:, slab(y)]
    pl.semaphore_wait(barrier, ROWS + COLS - 2)

    def band_push(i):
        chip = shifted(y, Y_STEPS[i], CHIPS_Y)
        return remote(
            own.at[:, slab(chip)], bands.at[r], band_send.at[i], band_recv.at[i], row=chip * 2 + core
        )

    def band_mate(i):
        ref = bands.at[r if i == 7 else shifted(y, -Y_STEPS[i], CHIPS_Y) * 2 + core]
        return remote(ref, ref, band_send.at[8 + i], band_recv.at[8 + i], row=y * 2 + 1 - core)

    for i in range(7):
        band_push(i).start()
    band_mate(7).start()
    for i in range(7):
        band_push(i).wait_recv()
        band_mate(i).start()
    for i in range(8):
        band_mate(i).wait_recv()

    lane = lax.broadcasted_iota(jnp.int32, (SLAB, 128), 1)

    def density(pair):
        v, w = val_index[pair], cond_index[pair]
        bra = bands[v, 0].astype(jnp.float32)
        ket = bands[w // 4, 1 + w % 4].astype(jnp.float32)
        gap = jnp.full((8, 128), cond_energy[w] - val_energy[v], jnp.float32)
        factor = jnp.sqrt(4.0 / gap) * (1.0 / 512)
        factor = jnp.concatenate([factor, factor], axis=0)
        same = bra * ket
        cross = bra * pltpu.roll(ket, 64, 1)
        real = same + pltpu.roll(same, 64, 1)
        imag = pltpu.roll(cross, 64, 1) - cross
        return (jnp.where(lane < 64, real, imag) * factor).astype(jnp.bfloat16)

    def produce(n, _):
        turn, first_col = lax.rem(n * 3, CHIPS_Y), (n // CHIPS_Y) * GROUP
        row = shifted(y, turn, CHIPS_Y) * 2 + core
        cols = [lax.rem(c + first_col + i, COLS) for i in range(GROUP)]
        for to in cols:
            staged[turn, to] = density(row * COLS + to)
        for i, to in enumerate(cols):
            copy = remote(
                staged.at[turn, to], dens.at[c, slab(y)], pair_send.at[turn], pair_recv.at[turn],
                row=row, col=to,
            )
            if i > 0:
                copy.start()
            else:
                @pl.when(n > 0)
                def _():
                    copy.start()

                @pl.when(n == 0)
                def _():
                    dens[c, slab(y)] = staged[0, c]
        return 0

    lax.fori_loop(0, CHIPS_Y * COLS // GROUP, produce, 0)

    def pair_group(turn):
        count = COLS - 1 if isinstance(turn, int) else COLS
        return remote(
            staged.at[turn, pl.ds(0, count)],
            dens.at[pl.ds(0, count), slab(shifted(y, -turn, CHIPS_Y))],
            pair_send.at[turn], pair_recv.at[turn],
            row=shifted(y, 1, CHIPS_Y) * 2 + core, col=c,
        )

    z_tab = z_table[...]
    left_tab = left_table[...]
    sign = jnp.where(lax.broadcasted_iota(jnp.int32, (64, 128), 1) < 64, 1.0, -1.0)

    def transform(parts):
        high = [p.astype(jnp.bfloat16) for p in parts]
        low = [(p - h.astype(jnp.float32)).astype(jnp.bfloat16) for p, h in zip(parts, high)]
        high = jnp.concatenate(high, axis=1)
        low = jnp.concatenate(low, axis=1)
        got = jnp.dot(
            left_tab, jnp.concatenate([high, high, low], axis=0), preferred_element_type=jnp.float32
        )
        return [
            got[:64, 128 * n : 128 * (n + 1)]
            + sign * pltpu.roll(got[64:, 128 * n : 128 * (n + 1)], 64, 1)
            for n in range(len(parts))
        ]

    def along_z(chip):
        part = dens[:, slab(chip)].reshape(COLS * SLAB, 128)
        got = jnp.dot(
            jnp.concatenate([part, part], axis=1), z_tab, preferred_element_type=jnp.float32
        )
        first[:, slab(chip)] = got.reshape(COLS, SLAB, 128)

    def arrived(turn, _):
        pair_group(turn).wait_recv()
        along_z(shifted(y, -turn, CHIPS_Y))
        return 0

    pair_group(0).wait_recv()
    along_z(y)
    lax.fori_loop(1, CHIPS_Y, arrived, 0)

    for plane in range(2):
        def along_y(i, _):
            got = transform([first[i * 8 + n, pl.ds(64 * plane, 64)] for n in range(8)])
            for n in range(8):
                base = pl.multiple_of((i * 8 + n) * 128 + 64 * plane, 64)
                second[pl.ds(base, 64), :] = got[n]
            return 0

        lax.fori_loop(0, 4, along_y, 0)

    for i in range(8):
        done = transform([second[pl.ds(i * 8 + n, 64, stride=64), :] for n in range(8)])
        for n in range(4):
            tile = jnp.concatenate(done[2 * n : 2 * n + 2], axis=0)
            number = i * 4 + n
            picked[
                pl.ds((number // 8) * 128, 128), pl.ds((number % 8) * 128, 128)
            ] = tile.T.astype(jnp.bfloat16)

    inner = lax.broadcasted_iota(jnp.int32, (1024, 1024), 0)
    outer = lax.broadcasted_iota(jnp.int32, (256, 1024), 0)

    def row_copy(b, h, rr):
        return remote(amp.at[b], row_land.at[h, r], row_send.at[b], row_recv.at[h, r], row=rr)

    def col_copy(b):
        return remote(amp.at[b], col_land.at[c], col_send.at[b], col_recv.at[c], col=b)

    def select(h):
        def step(t, _):
            blocks = (4 * t + h, 4 * t + 2 + h)
            spot = jnp.concatenate(
                [index[pl.ds(4 * b + i, 1), :] for b in blocks for i in range(4)], axis=1
            )
            kx, ky, kz = spot // 4096, (spot // 64) % 64, spot % 64
            hot = jnp.where(inner == (ky % 16) * 64 + kx, 1.0, 0.0).astype(jnp.bfloat16)
            got = jnp.dot(picked[...], hot, preferred_element_type=jnp.float32)
            keep = outer == (ky // 16) * 64 + kz
            for part in range(2):
                half = jnp.concatenate(
                    [got[128 * g + 64 * part : 128 * g + 64 * part + 64] for g in range(4)], axis=0
                )
                row = jnp.sum(jnp.where(keep, half, 0.0), axis=0, keepdims=True)
                for j in range(8):
                    amp[blocks[j // 4], pl.ds(4 * part + j % 4, 1), :] = row[:, 128 * j : 128 * (j + 1)]
            for n, b in enumerate(blocks):
                rr = 2 * t + n

                @pl.when(rr != r)
                def _():
                    row_copy(b, h, rr).start()

                @pl.when(rr == r)
                def _():
                    row_land[h, r] = amp[b]

                @pl.when(b != c)
                def _():
                    col_copy(b).start()

                @pl.when(b == c)
                def _():
                    col_land[c] = amp[b]
            return 0

        return step

    def row_half(h):
        def settle(k, _):
            origin = lax.rem(r - k + ROWS, ROWS)
            remote(
                amp.at[0], row_land.at[h, origin], row_send.at[0], row_recv.at[h, origin], row=origin
            ).wait_recv()
            return 0

        lax.fori_loop(1, ROWS, settle, 0)
        wide[pl.ds(0, 128), :] = row_land[h].reshape(128, 128)
        for j in range(8):
            left[h, x, z, j] = wide[pl.ds(j, 16, stride=8), :].astype(jnp.bfloat16)
        return ColGather(
            lambda xx, zz: left.at[h, xx, zz], lambda n: left_send.at[h, n], lambda n: left_recv.at[h, n]
        )

    lax.fori_loop(0, 8, select(0), 0)
    early = row_half(0)
    early.start()
    for low, high, ready in ((0, 2, (0, 1)), (2, 4, (2, 3)), (4, 6, (4, 5, 6)), (6, 8, ())):
        lax.fori_loop(low, high, select(1), 0)
        for i in ready:
            early.forward(i)
    late = row_half(1)
    late.start()

    def col_settle(k, _):
        origin = lax.rem(c - k + COLS, COLS)
        remote(
            amp.at[0], col_land.at[origin], col_send.at[0], col_recv.at[origin], col=origin
        ).wait_recv()
        return 0

    lax.fori_loop(1, COLS, col_settle, 0)
    wide[pl.ds(0, 256), :] = col_land[...].reshape(256, 128)
    for j in range(8):
        right[r, j] = wide[pl.ds(j, 32, stride=8), :].astype(jnp.bfloat16)
    column = RowGather(lambda slot: right.at[slot], lambda n: right_send.at[n], lambda n: right_recv.at[n])
    column.start()

    for i in range(7):
        band_push(i).wait_send()
    for i in range(8):
        band_mate(i).wait_send()

    def pair_end(turn, _):
        pair_group(turn).wait_send()
        return 0

    pair_group(0).wait_send()
    lax.fori_loop(1, CHIPS_Y, pair_end, 0)

    def amp_end(b, _):
        @pl.when(b // 2 != r)
        def _():
            row_copy(b, b % 2, b // 2).wait_send()

        @pl.when(b != c)
        def _():
            col_copy(b).wait_send()

        return 0

    lax.fori_loop(0, COLS, amp_end, 0)
    early.arrive()
    early.finish()

    for i in range(4):
        late.forward(i)
    column.middle()
    for i in range(4, 7):
        late.forward(i)
    column.end()

    wide[...] = right[...].reshape(4096, 128).astype(jnp.float32)

    def reorder(n, _):
        for q in range(8):
            rhs[
                pl.ds(pl.multiple_of((q // 4) * 512 + n * 16, 16), 16), pl.ds((q % 4) * 128, 128)
            ] = wide[pl.ds(q * 32 + n, 16, stride=256), :].astype(jnp.bfloat16)
        return 0

    lax.fori_loop(0, COLS, reorder, 0)

    late.arrive()
    late.finish()
    column.finish()


def window(val_index, cond_index, val_energy, cond_energy, own, index):
    z_table, left_table = tables()
    dma = pltpu.SemaphoreType.DMA
    f32, bf16 = jnp.float32, jnp.bfloat16
    return pl.pallas_call(
        window_kernel,
        out_shape=(
            jax.ShapeDtypeStruct((2, CHIPS_X, CHIPS_Z, 8, 16, 128), bf16),
            jax.ShapeDtypeStruct((1024, 512), bf16),
        ),
        in_specs=[SMEM] * 4 + [VMEM] * 4,
        out_specs=(VMEM, VMEM),
        scratch_shapes=[
            pltpu.VMEM((ROWS, BANDS_DEV, SLAB, 128), bf16),
            pltpu.VMEM((CHIPS_Y, COLS, SLAB, 128), bf16),
            pltpu.VMEM((COLS, 128, 128), bf16),
            pltpu.VMEM((COLS, 128, 128), f32),
            pltpu.VMEM((4096, 128), f32),
            pltpu.VMEM((512, 1024), bf16),
            pltpu.VMEM((COLS, 8, 128), f32),
            pltpu.VMEM((2, ROWS, 8, 128), f32),
            pltpu.VMEM((COLS, 8, 128), f32),
            pltpu.VMEM((ROWS, 8, COLS, 128), bf16),
            pltpu.VMEM((4096, 128), f32),
            dma((16,)), dma((16,)), dma((CHIPS_Y,)), dma((CHIPS_Y,)),
            dma((COLS,)), dma((2, ROWS)), dma((COLS,)), dma((COLS,)),
            dma((2, 31)), dma((2, 31)), dma((15,)), dma((15,)),
        ],
        compiler_params=pltpu.CompilerParams(
            collective_id=0, has_side_effects=True, vmem_limit_bytes=VMEM_LIMIT
        ),
        name="window",
    )(val_index, cond_index, val_energy, cond_energy, own, z_table, left_table, index)


def product_kernel(left, rhs, out):
    j = pl.program_id(0)
    real = left[j // 4, :, :, j % 4].reshape(512, 128).astype(jnp.float32).T.astype(jnp.bfloat16)
    imag = left[j // 4, :, :, j % 4 + 4].reshape(512, 128).astype(jnp.float32).T.astype(jnp.bfloat16)
    lhs = jnp.concatenate(
        [jnp.concatenate([real, imag], axis=1), jnp.concatenate([imag, -real], axis=1)], axis=0
    )
    got = jnp.dot(lhs, rhs[...], preferred_element_type=jnp.float32) * (-1.0 / 512)
    out[0] = got[:128]
    out[1] = got[128:]


def product(left, rhs):
    block = (1, CHIPS_X, CHIPS_Z, 1, 16, 128)
    return pl.pallas_call(
        product_kernel,
        grid=(8,),
        out_shape=jax.ShapeDtypeStruct((2, 1024, 512), jnp.float32),
        in_specs=[
            VMEM, VMEM,
        ],
        out_specs=pl.BlockSpec((2, 128, 512), lambda j: (0, j, 0)),
        compiler_params=pltpu.CompilerParams(vmem_limit_bytes=VMEM_LIMIT),
        name="product",
    )(left, rhs)


def local(val_waves, cond_waves, val_energy, cond_energy, val_index, cond_index, grid_index):
    waves = jnp.concatenate([val_waves, cond_waves], axis=1).reshape(2, BANDS_DEV, 2, GRID, GRID)
    own = jnp.transpose(waves, (1, 2, 3, 0, 4)).reshape(BANDS_DEV, 128, 128)
    left, rhs = window(
        val_index, cond_index, val_energy, cond_energy, own, grid_index.reshape(128, 128)
    )
    return product(left, rhs)


def solution(mesh):
    placed = (P(None, "row", "col", None), P(None, "row", "col", None), P(), P(), P(), P(), P())
    return jax.shard_map(
        local, mesh=mesh, in_specs=placed, out_specs=P(None, "row", "col"), check_vma=False
    )
```
